32 devices in a mesh: groups: 2 (over y), ep: 4 (over x, core), tp: 4 (over z).
Axes of the slice: x: 2, y: 2, z: 4, core: 2. Of those that a mesh axis runs over, the one named last changes fastest.
Arguments:
- tokens: bfloat16 [1024, 6144], P(('groups', 'ep'), 'tp'), parts along dimension 0, may hold values from -6 to 6
- picks: int32 [1024, 2], P(('groups', 'ep')), parts along dimension 0, may hold values from 0 to 3, all different within a row; in each aligned block of 128 rows (0 to 127, 128 to 255, ...) at most 80 rows name the same one
- gates: float32 [1024, 2], P(('groups', 'ep')), parts along dimension 0, may hold values from 0.1 to 1
- counts: int32 [8], P(('groups', 'ep')), parts along dimension 0, may hold values from 64 to 128, as said below
- gate_weight: bfloat16 [6144, 32768], P(None, ('ep', 'tp')), may hold values from -0.078125 to 0.078125
- up_weight: bfloat16 [6144, 32768], P(None, ('ep', 'tp')), may hold values from -0.078125 to 0.078125
- down_weight: bfloat16 [32768, 6144], P('ep', 'tp'), may hold values from -0.0625 to 0.0625
Outputs:
- mixed: bfloat16 [1024, 6144], P(('groups', 'ep'), 'tp'), parts along dimension 0
The draws below stay inside these ranges and needn't reach their ends.
There are 2 independent parts, one for each index of `groups`. The reference program is written for one: setup_inputs(seed, part) draws one part's arguments, and reference() takes and returns one part's arrays. A program takes and returns all parts, laid end to end along the dimension named above; an argument that names none is the same for every part. Nothing has to cross between parts.
Inputs may be any that keep to these rules, and one draw needn't show every extreme that they name: The two picks of a row differ; among the rows of one index of ep no expert is named by more than 80 rows. `counts`: some index of ep has all 128 rows valid; valid rows come first in each block.
All inputs are finite; a program needn't handle non-finite values.
Results may differ from the reference program's by a relative error of at most 0.005.
Values may be sent and summed in bfloat16 or wider, within the bound.
A program may use at most 192 MiB of HBM per device.

```python
import math
import jax
import jax.numpy as jnp
import numpy as np

D = 6144
FFW = 8192
E = 4
TOK_EP = 128
CAP = 80
TOKENS = 512
N_EP = 4


def draw_counts(key, part):
    key = jax.random.fold_in(key, 7)
    first_key, second_key = jax.random.split(key)
    values = jax.random.randint(first_key, (N_EP,), TOK_EP // 2, TOK_EP + 1)
    full_index = jax.random.randint(second_key, (), 0, N_EP)
    return jnp.where(jnp.arange(N_EP) == full_index, TOK_EP, values).astype(jnp.int32)


def shard_levels(rng, shape, pieces, low, largest):
    level = 1.0
    for position, shards_of in pieces:
        steps = jax.random.uniform(jax.random.fold_in(jax.random.fold_in(rng, 6), position), (shards_of,), jnp.float32, low / len(pieces), largest / len(pieces))
        level = level * jnp.repeat(jnp.exp(steps), shape[position] // shards_of).reshape((-1,) + (1,) * (len(shape) - 1 - position))
    return level


def assign_block(own_key, own, number, rows, count, top, most, slope):
    ranking = jax.random.permutation(own_key, count)
    packed, ordinary = shares(count, rows * top, most, slope, True), shares(count, rows * top, most, slope, False)
    places = jnp.arange(count)

    def named(tallies, turn):
        used = int((tallies > 0).sum())
        fixed = max(1, used // 4)
        moved = fixed + (places - fixed + turn * (used - fixed)) % max(1, count - fixed)
        return jnp.zeros((count,), jnp.int32).at[ranking[jnp.where(places < fixed, places, moved)]].set(jnp.asarray(tallies, jnp.int32))

    tallies = jnp.where(number % 4 == 0, named(packed, number // 4), named(ordinary, number - number // 4 - 1))
    mixed = jax.random.permutation(jax.random.fold_in(own, 3), count)
    donor, taker = mixed[0:count // 2 * 2:2], mixed[1:count // 2 * 2:2]
    slack = jnp.minimum(tallies[donor] - 1, most - tallies[taker]) // 2
    slack = jnp.where((donor == ranking[0]) | (taker == ranking[0]) | (tallies[taker] == 0), 0, jnp.maximum(slack, 0))
    moved = jax.random.randint(jax.random.fold_in(own, 4), (count // 2,), 0, 1 << 20) % (slack + 1)
    tallies = tallies.at[donor].add(-moved).at[taker].add(moved)
    labels = jnp.searchsorted(jnp.cumsum(tallies), jnp.arange(rows * top), side="right").astype(jnp.int32)
    grid = labels.reshape(top, rows).T
    grid = grid[jax.random.permutation(jax.random.fold_in(own, 1), rows)]
    turn = jax.random.randint(jax.random.fold_in(own, 2), (rows, 1), 0, top)
    return jnp.take_along_axis(grid, (jnp.arange(top)[None, :] + turn) % top, axis=1)


def shares(amount, total, bound, skew, full):
    weights = [(1 << 20) // math.isqrt(rank ** skew) + 1 for rank in range(1, amount + 1)]
    largest = bound if full else min(bound, max(-(-total // amount), total * weights[0] // sum(weights)))
    least = 1 if total - largest >= amount - 1 else 0
    holding, surplus = [largest] + [least] * (amount - 1), total - largest - least * (amount - 1)
    while surplus > 0:
        candidates = [i for i in range(1, amount) if holding[i] < largest] or [i for i in range(1, amount) if holding[i] < bound]
        pool, budget = sum([weights[i] for i in candidates]), surplus
        for i in candidates:
            addition = min(bound - holding[i], max(1, budget * weights[i] // pool), surplus)
            holding[i] = holding[i] + addition
            surplus = surplus - addition
    return np.array(holding)


def gaussian(key, shape, spread, most, pieces=(), held_as=jnp.bfloat16):
    entries = spread * jax.random.normal(key, shape, jnp.float32)
    if pieces:
        entries = entries * shard_levels(key, shape, pieces, -0.22, 0.18)
    return jnp.clip(entries, -most, most).astype(held_as)


def setup_inputs(seed: int = 0, part: int = 0) -> dict:
    key_of = jax.random.split(jax.random.key(seed), 8)
    own_keys = jax.random.split(jax.random.fold_in(key_of[7], part), 8)
    tokens = gaussian(own_keys[0], (TOKENS, D), 1.0, 6.0, ((0, 4), (1, 4)))
    picks_keys = jax.random.split(jax.random.fold_in(own_keys[1], 1), TOKENS // TOK_EP)
    picks_turns = jax.random.permutation(jax.random.fold_in(own_keys[1], 3), TOKENS // TOK_EP)
    picks = jax.vmap(lambda own, number: assign_block(jax.random.fold_in(own_keys[1], 2), own, number, TOK_EP, E, 2, CAP, 2))(picks_keys, picks_turns).reshape((TOKENS, 2))
    gates = jnp.clip(jnp.exp(math.log(1.0) - 2.3025851 * jax.random.uniform(own_keys[2], (TOKENS, 2), jnp.float32) ** shard_levels(own_keys[2], (TOKENS, 2), ((0, 4),), -0.2, 0.2)), 0.1, 1.0)
    counts = draw_counts(jax.random.fold_in(jax.random.fold_in(key_of[7], part), 71), part)
    gate_weight = gaussian(key_of[4], (D, E * FFW), D ** -0.5, 0.078125, ((1, 16),))
    up_weight = gaussian(key_of[5], (D, E * FFW), D ** -0.5, 0.078125, ((1, 16),))
    down_weight = gaussian(key_of[6], (E * FFW, D), FFW ** -0.5, 0.0625, ((0, 4), (1, 4)))
    return dict(tokens=tokens, picks=picks, gates=gates, counts=counts, gate_weight=gate_weight, up_weight=up_weight, down_weight=down_weight)


def reference(tokens, picks, gates, counts, gate_weight, up_weight, down_weight):
    row_ids = jnp.arange(TOKENS, dtype=jnp.int32)
    blocks = (row_ids // TOK_EP).astype(jnp.int32)
    live_rows = ((row_ids % TOK_EP) < counts[blocks]).astype(gates.dtype)
    total = jnp.zeros((TOKENS, D), jnp.float32)
    for expert in range(E):
        weight = jnp.sum(jnp.where(picks == expert, gates, jnp.zeros_like(gates)), axis=1) * live_rows
        gate_cols = gate_weight[:, expert * FFW:(expert + 1) * FFW]
        up_cols = up_weight[:, expert * FFW:(expert + 1) * FFW]
        pre_gate = jnp.dot(tokens, gate_cols, preferred_element_type=jnp.float32)
        pre_up = jnp.dot(tokens, up_cols, preferred_element_type=jnp.float32)
        hidden = (jax.nn.silu(pre_gate) * pre_up).astype(jnp.bfloat16)
        down_rows = down_weight[expert * FFW:(expert + 1) * FFW, :]
        output = jnp.dot(hidden, down_rows, preferred_element_type=jnp.float32)
        total = total + weight[:, None].astype(jnp.float32) * output
    return total.astype(jnp.bfloat16)
```

```python
import functools

import jax
import jax.numpy as jnp
from jax import lax
from jax.experimental import pallas as pl
from jax.experimental.pallas import tpu as pltpu
from jax.sharding import PartitionSpec as P

E = 4
CAP = 80
MESH = pl.DeviceIdType.MESH


def gather_kernel(n_ep, n_tp, halves, tok, meta, out, meta_out, local_sem, z_send, x_send, c_send, recv, m_send, m_recv):
    z = lax.axis_index("tp")
    b = lax.axis_index("ep")
    chips = n_ep // 2
    rows, width = tok.shape
    part_rows = rows // halves
    partner = b + 1 - 2 * lax.rem(b, 2)
    peers = [2 * lax.rem(b // 2 + j, chips) + lax.rem(b, 2) for j in range(1, chips)]
    others = [lax.rem(b + j, n_ep) for j in range(1, n_ep)]

    def piece(block, p, h):
        return out.at[block, pl.ds(h * part_rows, part_rows), pl.ds(pl.multiple_of(p * width, 128), width)]

    def copy(block, p, h, own, send, device):
        src = tok.at[pl.ds(h * part_rows, part_rows), :] if own else piece(block, p, h)
        return pltpu.make_async_remote_copy(
            src_ref=src, dst_ref=piece(block, p, h), send_sem=send, recv_sem=recv.at[block, p, h],
            device_id=device, device_id_type=MESH)

    def right(p, h, own=False):
        return copy(b, p, h, own, z_send.at[0, p, h], {"tp": z + 1})

    def left(p, h, own=False):
        return copy(b, p, h, own, z_send.at[1, p, h], {"tp": z - 1})

    def across(j, p, h, own=False):
        return copy(b, p, h, own, x_send.at[j, p, h], {"ep": peers[j]})

    def to_core(block, p, h, own=False):
        return copy(block, p, h, own, c_send.at[block, p, h], {"ep": partner})

    def meta_copy(j):
        return pltpu.make_async_remote_copy(
            src_ref=meta, dst_ref=meta_out.at[b], send_sem=m_send.at[j], recv_sem=m_recv.at[b],
            device_id={"ep": others[j]}, device_id_type=MESH)

    local = pltpu.make_async_copy(tok, out.at[b, :, pl.ds(pl.multiple_of(z * width, 128), width)], local_sem.at[0])
    local_meta = pltpu.make_async_copy(meta, meta_out.at[b], local_sem.at[1])

    barrier = pltpu.get_barrier_semaphore()
    for other in others:
        pl.semaphore_signal(barrier, inc=1, device_id={"ep": other}, device_id_type=MESH)

    @pl.when(z > 0)
    def _():
        pl.semaphore_signal(barrier, inc=1, device_id={"tp": z - 1}, device_id_type=MESH)

    @pl.when(z < n_tp - 1)
    def _():
        pl.semaphore_signal(barrier, inc=1, device_id={"tp": z + 1}, device_id_type=MESH)

    pl.semaphore_wait(barrier, n_ep - 1 + jnp.minimum(z, 1) + jnp.minimum(n_tp - 1 - z, 1))

    def fan_out(p, h, own):
        for j in range(chips - 1):
            across(j, p, h, own).start()
        to_core(b, p, h, own).start()

    for h in range(halves):
        @pl.when(z < n_tp - 1)
        def _():
            right(z, h, True).start()

        @pl.when(z > 0)
        def _():
            left(z, h, True).start()

        fan_out(z, h, True)
    for j in range(n_ep - 1):
        meta_copy(j).start()
    local.start()
    local_meta.start()

    def pass_to_core(k, h):
        for p, there in ((z - k, z - k >= 0), (z + k, z + k < n_tp))[: 1 if k == 0 else 2]:
            @pl.when(there)
            def _():
                for block in peers:
                    to_core(block, p, h).wait_recv()
                    to_core(block, p, h).start()

    for k in range(1, n_tp):
        for h in range(halves):
            @pl.when(z - k >= 0)
            def _():
                right(z - k, h).wait_recv()

                @pl.when(z < n_tp - 1)
                def _():
                    right(z - k, h).start()

                fan_out(z - k, h, False)

            @pl.when(z + k < n_tp)
            def _():
                left(z + k, h).wait_recv()

                @pl.when(z > 0)
                def _():
                    left(z + k, h).start()

                fan_out(z + k, h, False)

            pass_to_core(k - 1, h)
    for h in range(halves):
        pass_to_core(n_tp - 1, h)

    for p in range(n_tp):
        for h in range(halves):
            for block in [partner] + [peer + partner - b for peer in peers]:
                to_core(block, p, h).wait_recv()
            for block in [b] + peers:
                to_core(block, p, h).wait_send()
            for j in range(chips - 1):
                across(j, p, h).wait_send()

            @pl.when((z < n_tp - 1) & (p <= z))
            def _():
                right(p, h).wait_send()

            @pl.when((z > 0) & (p >= z))
            def _():
                left(p, h).wait_send()
    for j in range(n_ep - 1):
        meta_copy(j).wait_send()
        pltpu.make_async_remote_copy(
            src_ref=meta, dst_ref=meta_out.at[others[j]], send_sem=m_send.at[j], recv_sem=m_recv.at[others[j]],
            device_id={"ep": others[j]}, device_id_type=MESH).wait_recv()
    local.wait()
    local_meta.wait()


def gather_tokens(tokens, meta, n_ep, n_tp):
    rows, width = tokens.shape
    halves = 2 if n_ep * n_tp <= 16 else 1
    dma = pltpu.SemaphoreType.DMA
    hbm = pl.BlockSpec(memory_space=pl.ANY)
    return pl.pallas_call(
        functools.partial(gather_kernel, n_ep, n_tp, halves),
        out_shape=(jax.ShapeDtypeStruct((n_ep, rows, n_tp * width), tokens.dtype),
                   jax.ShapeDtypeStruct((n_ep,) + meta.shape, meta.dtype)),
        in_specs=[hbm, hbm],
        out_specs=(hbm, hbm),
        scratch_shapes=[dma((2,)), dma((2, n_tp, halves)), dma((max(1, n_ep // 2 - 1), n_tp, halves)),
                        dma((n_ep, n_tp, halves)), dma((n_ep, n_tp, halves)), dma((n_ep,)), dma((n_ep,))],
        compiler_params=pltpu.CompilerParams(collective_id=0, has_side_effects=True),
        name="gather_tokens",
    )(tokens, meta)


def ffn_kernel(n_tp, cols, x, gate, up, down, out, wg, wu, wd, hid, acc, w_sem, d_sem, r_send, l_send, recv):
    z = lax.axis_index("tp")
    steps = hid.shape[1]
    depth = steps * cols

    def fetch(c, slot):
        at = pl.ds(pl.multiple_of(c * cols, 128), cols)
        return (pltpu.make_async_copy(gate.at[:, at], wg.at[slot], w_sem.at[0, slot]),
                pltpu.make_async_copy(up.at[:, at], wu.at[slot], w_sem.at[1, slot]))

    def fetch_down(s):
        at = pl.ds(pl.multiple_of(s * depth, 128), depth)
        return pltpu.make_async_copy(down.at[at, :], wd.at[at, :], d_sem.at[s])

    def send(s, c, sem, to):
        return pltpu.make_async_remote_copy(
            src_ref=hid.at[s, c], dst_ref=hid.at[s, c], send_sem=sem.at[s, c], recv_sem=recv.at[s, c],
            device_id={"tp": to}, device_id_type=MESH)

    def right(s, c):
        return send(s, c, r_send, z + 1)

    def left(s, c):
        return send(s, c, l_send, z - 1)

    for copy in fetch(0, 0):
        copy.start()
    acc[...] = jnp.zeros_like(acc)

    barrier = pltpu.get_barrier_semaphore()

    @pl.when(z > 0)
    def _():
        pl.semaphore_signal(barrier, inc=1, device_id={"tp": z - 1}, device_id_type=MESH)

    @pl.when(z < n_tp - 1)
    def _():
        pl.semaphore_signal(barrier, inc=1, device_id={"tp": z + 1}, device_id_type=MESH)

    pl.semaphore_wait(barrier, jnp.minimum(z, 1) + jnp.minimum(n_tp - 1 - z, 1))

    @pl.loop(0, steps)
    def _(c):
        slot = lax.rem(c, 2)

        @pl.when(c + 1 < steps)
        def _():
            for copy in fetch(c + 1, 1 - slot):
                copy.start()

        for copy in fetch(c, slot):
            copy.wait()
        pre_gate = jnp.dot(x[...], wg[slot], preferred_element_type=jnp.float32)
        pre_up = jnp.dot(x[...], wu[slot], preferred_element_type=jnp.float32)
        hid[z, c] = (pre_gate / (1.0 + jnp.exp(-pre_gate)) * pre_up).astype(hid.dtype)

        @pl.when(z < n_tp - 1)
        def _():
            right(z, c).start()

        @pl.when(z > 0)
        def _():
            left(z, c).start()

        @pl.when(c == max(0, steps - 2))
        def _():
            for s in range(n_tp):
                fetch_down(s).start()

    for s in range(n_tp):
        fetch_down(s).wait()

    def add(s, c):
        at = pl.ds(pl.multiple_of(s * depth + c * cols, 128), cols)
        acc[...] += jnp.dot(hid[s, c], wd[at, :], preferred_element_type=jnp.float32)

    for k in range(1, n_tp):
        @pl.loop(0, steps)
        def _(c):
            @pl.when(z - k >= 0)
            def _():
                right(z - k, c).wait_recv()

                @pl.when(z < n_tp - 1)
                def _():
                    right(z - k, c).start()

            @pl.when(z + k < n_tp)
            def _():
                left(z + k, c).wait_recv()

                @pl.when(z > 0)
                def _():
                    left(z + k, c).start()

            if k == 1:
                add(z, c)

            @pl.when(z - k >= 0)
            def _():
                add(z - k, c)

            @pl.when(z + k < n_tp)
            def _():
                add(z + k, c)

    out[...] = acc[...].astype(out.dtype)

    @pl.loop(0, steps)
    def _(c):
        for s in range(n_tp):
            @pl.when((z < n_tp - 1) & (s <= z))
            def _():
                right(s, c).wait_send()

            @pl.when((z > 0) & (s >= z))
            def _():
                left(s, c).wait_send()


def ffn(x, gate, up, down, n_tp):
    rows, width = x.shape
    hidden = gate.shape[1]
    cols = min(256, hidden)
    steps = hidden // cols
    dma = pltpu.SemaphoreType.DMA
    hbm = pl.BlockSpec(memory_space=pl.ANY)
    vmem = pl.BlockSpec(memory_space=pltpu.VMEM)
    bf16 = jnp.bfloat16
    return pl.pallas_call(
        functools.partial(ffn_kernel, n_tp, cols),
        out_shape=jax.ShapeDtypeStruct((rows, down.shape[1]), bf16),
        in_specs=[vmem, hbm, hbm, hbm],
        out_specs=vmem,
        scratch_shapes=[
            pltpu.VMEM((2, width, cols), bf16), pltpu.VMEM((2, width, cols), bf16),
            pltpu.VMEM(down.shape, bf16),
            pltpu.VMEM((n_tp, steps, rows, cols), bf16),
            pltpu.VMEM((rows, down.shape[1]), jnp.float32),
            dma((2, 2)), dma((n_tp,)), dma((n_tp, steps)), dma((n_tp, steps)), dma((n_tp, steps))],
        compiler_params=pltpu.CompilerParams(
            collective_id=1, has_side_effects=True, vmem_limit_bytes=60 * 1024 * 1024),
        cost_estimate=pl.CostEstimate(
            flops=2 * rows * (2 * width * hidden + down.size),
            bytes_accessed=2 * (gate.size + up.size + down.size), transcendentals=rows * hidden),
        name="ffn",
    )(x, gate, up, down)


def body(tokens, picks, gates, counts, gate_weight, up_weight, down_weight):
    n_ep, n_tp = lax.axis_size("ep"), lax.axis_size("tp")
    copies = n_ep // E
    row_count = tokens.shape[0]
    live = jnp.arange(row_count) < counts[0]
    meta = jnp.full((8, row_count), -1, jnp.int32).at[:2].set(jnp.where(live[None], picks.T, -1))
    gathered, meta_all = gather_tokens(tokens, meta, n_ep, n_tp)
    slots = jnp.arange(CAP, dtype=jnp.int32)

    expert = lax.axis_index("ep") // copies
    routed = jnp.any(meta_all[:, :2] == expert, axis=1)
    rank = jnp.cumsum(routed.astype(jnp.int32), axis=1) - 1
    onehot = (routed[:, None] & (rank[:, None] == slots[None, :, None])).astype(jnp.bfloat16)
    packed = jnp.einsum("bcr,brf->bcf", onehot, gathered, preferred_element_type=jnp.float32)
    packed = packed.astype(jnp.bfloat16).reshape(n_ep * CAP, -1)

    partial_value = ffn(packed, gate_weight, up_weight, down_weight, n_tp)
    returned = lax.all_to_all(
        partial_value.reshape(n_ep, CAP, -1), "ep", split_axis=0, concat_axis=0, tiled=True)

    matches = picks[:, :, None] == jnp.arange(E, dtype=jnp.int32)
    own_routed = jnp.any(matches, axis=1) & live[:, None]
    row_weight = jnp.sum(jnp.where(matches, gates[:, :, None], 0.0), axis=1)
    own_rank = jnp.cumsum(own_routed.astype(jnp.int32), axis=0) - 1
    placed = (own_routed.T[:, None] & (own_rank.T[:, None] == slots[None, :, None]))
    combine = placed.astype(jnp.float32) * row_weight.T[:, None, :]
    summed = jnp.sum(returned.reshape(E, copies, CAP, -1).astype(jnp.float32), axis=1)
    mixed = jnp.einsum("ecr,ecf->rf", combine, summed, precision=lax.Precision.HIGHEST)
    return mixed.astype(jnp.bfloat16)


def solution(mesh):
    rows = P(("groups", "ep"), None)
    in_specs = (
        P(("groups", "ep"), "tp"), rows, rows, P(("groups", "ep")),
        P(None, ("ep", "tp")), P(None, ("ep", "tp")), P("ep", "tp"),
    )
    out_specs = P(("groups", "ep"), "tp")
    return jax.shard_map(body, mesh=mesh, in_specs=in_specs, out_specs=out_specs, check_vma=False)
```

```python
import functools

import jax
import jax.numpy as jnp
from jax import lax
from jax.experimental import pallas as pl
from jax.experimental.pallas import tpu as pltpu
from jax.sharding import PartitionSpec as P

E = 4
CAP = 80
MESH = pl.DeviceIdType.MESH


def gather_kernel(n_ep, n_tp, halves, tok, meta, out, meta_out, local_sem, z_send, x_send, c_send, recv, m_send, m_recv):
    z = lax.axis_index("tp")
    b = lax.axis_index("ep")
    chips = n_ep // 2
    rows, width = tok.shape
    part_rows = rows // halves
    partner = b + 1 - 2 * lax.rem(b, 2)
    peers = [2 * lax.rem(b // 2 + j, chips) + lax.rem(b, 2) for j in range(1, chips)]
    others = [lax.rem(b + j, n_ep) for j in range(1, n_ep)]

    def piece(block, p, h):
        return out.at[block, pl.ds(h * part_rows, part_rows), pl.ds(pl.multiple_of(p * width, 128), width)]

    def copy(block, p, h, own, send, device):
        src = tok.at[pl.ds(h * part_rows, part_rows), :] if own else piece(block, p, h)
        return pltpu.make_async_remote_copy(
            src_ref=src, dst_ref=piece(block, p, h), send_sem=send, recv_sem=recv.at[block, p, h],
            device_id=device, device_id_type=MESH)

    def right(p, h, own=False):
        return copy(b, p, h, own, z_send.at[0, p, h], {"tp": z + 1})

    def left(p, h, own=False):
        return copy(b, p, h, own, z_send.at[1, p, h], {"tp": z - 1})

    def across(j, p, h, own=False):
        return copy(b, p, h, own, x_send.at[j, p, h], {"ep": peers[j]})

    def to_core(block, p, h, own=False):
        return copy(block, p, h, own, c_send.at[block, p, h], {"ep": partner})

    def meta_copy(j):
        return pltpu.make_async_remote_copy(
            src_ref=meta, dst_ref=meta_out.at[b], send_sem=m_send.at[j], recv_sem=m_recv.at[b],
            device_id={"ep": others[j]}, device_id_type=MESH)

    local = pltpu.make_async_copy(tok, out.at[b, :, pl.ds(pl.multiple_of(z * width, 128), width)], local_sem.at[0])
    local_meta = pltpu.make_async_copy(meta, meta_out.at[b], local_sem.at[1])

    barrier = pltpu.get_barrier_semaphore()
    for other in others:
        pl.semaphore_signal(barrier, inc=1, device_id={"ep": other}, device_id_type=MESH)

    @pl.when(z > 0)
    def _():
        pl.semaphore_signal(barrier, inc=1, device_id={"tp": z - 1}, device_id_type=MESH)

    @pl.when(z < n_tp - 1)
    def _():
        pl.semaphore_signal(barrier, inc=1, device_id={"tp": z + 1}, device_id_type=MESH)

    pl.semaphore_wait(barrier, n_ep - 1 + jnp.minimum(z, 1) + jnp.minimum(n_tp - 1 - z, 1))

    def fan_out(p, h, own):
        for j in range(chips - 1):
            across(j, p, h, own).start()
        to_core(b, p, h, own).start()

    for h in range(halves):
        @pl.when(z < n_tp - 1)
        def _():
            right(z, h, True).start()

        @pl.when(z > 0)
        def _():
            left(z, h, True).start()

        fan_out(z, h, True)
    for j in range(n_ep - 1):
        meta_copy(j).start()
    local.start()
    local_meta.start()

    def pass_to_core(k, h):
        for p, there in ((z - k, z - k >= 0), (z + k, z + k < n_tp))[: 1 if k == 0 else 2]:
            @pl.when(there)
            def _():
                for block in peers:
                    to_core(block, p, h).wait_recv()
                    to_core(block, p, h).start()

    for k in range(1, n_tp):
        for h in range(halves):
            @pl.when(z - k >= 0)
            def _():
                right(z - k, h).wait_recv()

                @pl.when(z < n_tp - 1)
                def _():
                    right(z - k, h).start()

                fan_out(z - k, h, False)

            @pl.when(z + k < n_tp)
            def _():
                left(z + k, h).wait_recv()

                @pl.when(z > 0)
                def _():
                    left(z + k, h).start()

                fan_out(z + k, h, False)

            pass_to_core(k - 1, h)
    for h in range(halves):
        pass_to_core(n_tp - 1, h)

    for p in range(n_tp):
        for h in range(halves):
            for block in [partner] + [peer + partner - b for peer in peers]:
                to_core(block, p, h).wait_recv()
            for block in [b] + peers:
                to_core(block, p, h).wait_send()
            for j in range(chips - 1):
                across(j, p, h).wait_send()

            @pl.when((z < n_tp - 1) & (p <= z))
            def _():
                right(p, h).wait_send()

            @pl.when((z > 0) & (p >= z))
            def _():
                left(p, h).wait_send()
    for j in range(n_ep - 1):
        meta_copy(j).wait_send()
        pltpu.make_async_remote_copy(
            src_ref=meta, dst_ref=meta_out.at[others[j]], send_sem=m_send.at[j], recv_sem=m_recv.at[others[j]],
            device_id={"ep": others[j]}, device_id_type=MESH).wait_recv()
    local.wait()
    local_meta.wait()


def gather_tokens(tokens, meta, n_ep, n_tp):
    rows, width = tokens.shape
    halves = 2 if n_ep * n_tp <= 16 else 1
    dma = pltpu.SemaphoreType.DMA
    hbm = pl.BlockSpec(memory_space=pl.ANY)
    return pl.pallas_call(
        functools.partial(gather_kernel, n_ep, n_tp, halves),
        out_shape=(jax.ShapeDtypeStruct((n_ep, rows, n_tp * width), tokens.dtype),
                   jax.ShapeDtypeStruct((n_ep,) + meta.shape, meta.dtype)),
        in_specs=[hbm, hbm],
        out_specs=(hbm, hbm),
        scratch_shapes=[dma((2,)), dma((2, n_tp, halves)), dma((max(1, n_ep // 2 - 1), n_tp, halves)),
                        dma((n_ep, n_tp, halves)), dma((n_ep, n_tp, halves)), dma((n_ep,)), dma((n_ep,))],
        compiler_params=pltpu.CompilerParams(collective_id=0, has_side_effects=True),
        name="gather_tokens",
    )(tokens, meta)


def ffn_kernel(n_ep, n_tp, cols, tokens, onehot, gate, up, down, ret, x, held, wg, wu, wd, hid, acc, done,
               t_sem, w_sem, d_sem, r_send, l_send, recv, b_send, b_recv, o_send, o_recv):
    z = lax.axis_index("tp")
    b = lax.axis_index("ep")
    chips = n_ep // 2
    others = [lax.rem(b + j, n_ep) for j in range(1, n_ep)]
    steps = hid.shape[1]
    depth = steps * cols
    width = x.shape[1]
    strip = width // 4

    def order(i):
        return 2 * lax.rem(b // 2 + 1 + i // 2, chips) + lax.rem(b + 1 + i, 2)

    def rows_of(block):
        return pl.ds(pl.multiple_of(block * CAP, 16), CAP)

    def fetch(c, slot):
        at = pl.ds(pl.multiple_of(c * cols, 128), cols)
        return (pltpu.make_async_copy(gate.at[:, at], wg.at[slot], w_sem.at[0, slot]),
                pltpu.make_async_copy(up.at[:, at], wu.at[slot], w_sem.at[1, slot]))

    def fetch_down(s):
        at = pl.ds(pl.multiple_of(s * depth, 128), depth)
        return pltpu.make_async_copy(down.at[at, :], wd.at[at, :], d_sem.at[s])

    def fetch_tokens(block, slot):
        return pltpu.make_async_copy(tokens.at[block], held.at[slot], t_sem.at[slot])

    def send(s, c, sem, to):
        return pltpu.make_async_remote_copy(
            src_ref=hid.at[s, c], dst_ref=hid.at[s, c], send_sem=sem.at[s, c], recv_sem=recv.at[s, c],
            device_id={"tp": to}, device_id_type=MESH)

    def right(s, c):
        return send(s, c, r_send, z + 1)

    def left(s, c):
        return send(s, c, l_send, z - 1)

    def block_send(s, block, way, to):
        at = hid.at[s, :, rows_of(block), :]
        return pltpu.make_async_remote_copy(
            src_ref=at, dst_ref=at, send_sem=b_send.at[way, block], recv_sem=b_recv.at[block],
            device_id={"tp": to}, device_id_type=MESH)

    def back(block, source):
        return pltpu.make_async_remote_copy(
            src_ref=done.at[block], dst_ref=ret.at[source], send_sem=o_send.at[block], recv_sem=o_recv.at[source],
            device_id={"ep": block}, device_id_type=MESH)

    fetch_tokens(0, 0).start()
    for copy in fetch(0, 0):
        copy.start()

    barrier = pltpu.get_barrier_semaphore()
    for other in others:
        pl.semaphore_signal(barrier, inc=1, device_id={"ep": other}, device_id_type=MESH)

    @pl.when(z > 0)
    def _():
        pl.semaphore_signal(barrier, inc=1, device_id={"tp": z - 1}, device_id_type=MESH)

    @pl.when(z < n_tp - 1)
    def _():
        pl.semaphore_signal(barrier, inc=1, device_id={"tp": z + 1}, device_id_type=MESH)

    @pl.loop(0, n_ep)
    def _(block):
        slot = lax.rem(block, 2)

        @pl.when(block + 1 < n_ep)
        def _():
            fetch_tokens(block + 1, 1 - slot).start()

        fetch_tokens(block, slot).wait()
        for j in range(4):
            at = pl.ds(j * strip, strip)
            x[rows_of(block), at] = jnp.dot(
                onehot[block], held[slot, :, at], preferred_element_type=jnp.float32).astype(x.dtype)

    acc[...] = jnp.zeros_like(acc)
    pl.semaphore_wait(barrier, n_ep - 1 + jnp.minimum(z, 1) + jnp.minimum(n_tp - 1 - z, 1))

    @pl.loop(0, steps)
    def _(c):
        slot = lax.rem(c, 2)

        @pl.when(c + 1 < steps)
        def _():
            for copy in fetch(c + 1, 1 - slot):
                copy.start()

        for copy in fetch(c, slot):
            copy.wait()
        pre_gate = jnp.dot(x[...], wg[slot], preferred_element_type=jnp.float32)
        pre_up = jnp.dot(x[...], wu[slot], preferred_element_type=jnp.float32)
        hid[z, c] = (pre_gate / (1.0 + jnp.exp(-pre_gate)) * pre_up).astype(hid.dtype)

        @pl.when(z < n_tp - 1)
        def _():
            right(z, c).start()

        @pl.when(z > 0)
        def _():
            left(z, c).start()

        @pl.when(c == max(0, steps - 2))
        def _():
            for s in range(n_tp):
                fetch_down(s).start()

    def weights_of(s, c):
        return wd[pl.ds(pl.multiple_of(s * depth + c * cols, 128), cols), :]

    def add(s, c):
        acc[...] += jnp.dot(hid[s, c], weights_of(s, c), preferred_element_type=jnp.float32)

    def finish(i):
        block = order(i)
        value = acc[rows_of(block), :].astype(ret.dtype)
        if i == n_ep - 1:
            ret[b] = value
        else:
            done[block] = value
            back(block, b).start()

    for k in range(1, n_tp - 1):
        @pl.loop(0, steps)
        def _(c):
            @pl.when(z - k >= 0)
            def _():
                right(z - k, c).wait_recv()

                @pl.when(z < n_tp - 1)
                def _():
                    if k < n_tp - 2:
                        right(z - k, c).start()
                    else:
                        @pl.when(c == steps - 1)
                        def _():
                            for i in range(n_ep):
                                block_send(z - k, order(i), 0, z + 1).start()

            @pl.when(z + k < n_tp)
            def _():
                left(z + k, c).wait_recv()

                @pl.when(z > 0)
                def _():
                    if k < n_tp - 2:
                        left(z + k, c).start()
                    else:
                        @pl.when(c == steps - 1)
                        def _():
                            for i in range(n_ep):
                                block_send(z + k, order(i), 1, z - 1).start()

            if k == 1:
                @pl.when(c == 0)
                def _():
                    for s in range(n_tp):
                        fetch_down(s).wait()

                add(z, c)

            @pl.when(z - k >= 0)
            def _():
                add(z - k, c)

            @pl.when(z + k < n_tp)
            def _():
                add(z + k, c)

    at_end = (z == 0) | (z == n_tp - 1)

    @pl.when(at_end)
    def _():
        far = n_tp - 1 - z
        for i in range(n_ep):
            block = order(i)
            block_send(far, block, 0, jnp.where(z == 0, 1, z - 1)).wait_recv()

            @pl.loop(0, steps)
            def _(c):
                acc[rows_of(block), :] += jnp.dot(
                    hid[far, c, rows_of(block), :], weights_of(far, c), preferred_element_type=jnp.float32)

            finish(i)

    @pl.when(jnp.logical_not(at_end))
    def _():
        for i in range(n_ep):
            finish(i)

    @pl.loop(0, steps)
    def _(c):
        for s in range(n_tp):
            @pl.when((z < n_tp - 1) & (s <= z) & ((s > 0) | (z < n_tp - 2)))
            def _():
                right(s, c).wait_send()

            @pl.when((z > 0) & (s >= z) & ((s < n_tp - 1) | (z > 1)))
            def _():
                left(s, c).wait_send()

    for i in range(n_ep):
        @pl.when(z == n_tp - 2)
        def _():
            block_send(0, order(i), 0, z + 1).wait_send()

        @pl.when(z == 1)
        def _():
            block_send(n_tp - 1, order(i), 1, z - 1).wait_send()

    for other in others:
        back(other, other).wait_recv()
        back(other, b).wait_send()


def ffn(tokens, onehot, gate, up, down, n_ep, n_tp):
    width, hidden = gate.shape
    rows = n_ep * CAP
    out_width = down.shape[1]
    cols = min(256, hidden)
    steps = hidden // cols
    dma = pltpu.SemaphoreType.DMA
    hbm = pl.BlockSpec(memory_space=pl.ANY)
    vmem = pl.BlockSpec(memory_space=pltpu.VMEM)
    bf16 = jnp.bfloat16
    return pl.pallas_call(
        functools.partial(ffn_kernel, n_ep, n_tp, cols),
        out_shape=jax.ShapeDtypeStruct((n_ep, CAP, out_width), bf16),
        in_specs=[hbm, vmem, hbm, hbm, hbm],
        out_specs=vmem,
        scratch_shapes=[
            pltpu.VMEM((rows, width), bf16),
            pltpu.VMEM((2,) + tokens.shape[1:], bf16),
            pltpu.VMEM((2, width, cols), bf16), pltpu.VMEM((2, width, cols), bf16),
            pltpu.VMEM(down.shape, bf16),
            pltpu.VMEM((n_tp, steps, rows, cols), bf16),
            pltpu.VMEM((rows, out_width), jnp.float32),
            pltpu.VMEM((n_ep, CAP, out_width), bf16),
            dma((2,)), dma((2, 2)), dma((n_tp,)), dma((n_tp, steps)), dma((n_tp, steps)), dma((n_tp, steps)),
            dma((2, n_ep)), dma((n_ep,)), dma((n_ep,)), dma((n_ep,))],
        compiler_params=pltpu.CompilerParams(
            collective_id=1, has_side_effects=True, vmem_limit_bytes=60 * 1024 * 1024),
        cost_estimate=pl.CostEstimate(
            flops=2 * rows * (2 * width * hidden + down.size),
            bytes_accessed=2 * (gate.size + up.size + down.size), transcendentals=rows * hidden),
        name="ffn",
    )(tokens, onehot, gate, up, down)


def body(tokens, picks, gates, counts, gate_weight, up_weight, down_weight):
    n_ep, n_tp = lax.axis_size("ep"), lax.axis_size("tp")
    copies = n_ep // E
    row_count = tokens.shape[0]
    live = jnp.arange(row_count) < counts[0]
    meta = jnp.full((8, row_count), -1, jnp.int32).at[:2].set(jnp.where(live[None], picks.T, -1))
    gathered, meta_all = gather_tokens(tokens, meta, n_ep, n_tp)
    slots = jnp.arange(CAP, dtype=jnp.int32)

    expert = lax.axis_index("ep") // copies
    routed = jnp.any(meta_all[:, :2] == expert, axis=1)
    rank = jnp.cumsum(routed.astype(jnp.int32), axis=1) - 1
    onehot = (routed[:, None] & (rank[:, None] == slots[None, :, None])).astype(jnp.bfloat16)
    returned = ffn(gathered, onehot, gate_weight, up_weight, down_weight, n_ep, n_tp)

    matches = picks[:, :, None] == jnp.arange(E, dtype=jnp.int32)
    own_routed = jnp.any(matches, axis=1) & live[:, None]
    row_weight = jnp.sum(jnp.where(matches, gates[:, :, None], 0.0), axis=1)
    own_rank = jnp.cumsum(own_routed.astype(jnp.int32), axis=0) - 1
    placed = (own_routed.T[:, None] & (own_rank.T[:, None] == slots[None, :, None]))
    combine = placed.astype(jnp.float32) * row_weight.T[:, None, :]
    summed = jnp.sum(returned.reshape(E, copies, CAP, -1).astype(jnp.float32), axis=1)
    mixed = jnp.einsum("ecr,ecf->rf", combine, summed, precision=lax.Precision.HIGHEST)
    return mixed.astype(jnp.bfloat16)


def solution(mesh):
    rows = P(("groups", "ep"), None)
    in_specs = (
        P(("groups", "ep"), "tp"), rows, rows, P(("groups", "ep")),
        P(None, ("ep", "tp")), P(None, ("ep", "tp")), P("ep", "tp"),
    )
    out_specs = P(("groups", "ep"), "tp")
    return jax.shard_map(body, mesh=mesh, in_specs=in_specs, out_specs=out_specs, check_vma=False)
```

```python
import functools

import jax
import jax.numpy as jnp
from jax import lax
from jax.experimental import pallas as pl
from jax.experimental.pallas import tpu as pltpu
from jax.sharding import PartitionSpec as P

E = 4
CAP = 80
MESH = pl.DeviceIdType.MESH


def gather_kernel(n_ep, n_tp, halves, tok, meta, out, meta_out, local_sem, z_send, turn_send, x_send, c_send, recv, m_send, m_recv):
    z = lax.axis_index("tp")
    b = lax.axis_index("ep")
    chips = n_ep // 2
    rows, width = tok.shape
    part_rows = rows // halves
    partner = b + 1 - 2 * lax.rem(b, 2)
    peers = [2 * lax.rem(b // 2 + j, chips) + lax.rem(b, 2) for j in range(1, chips)]
    others = [lax.rem(b + j, n_ep) for j in range(1, n_ep)]

    def piece(block, p, h):
        return out.at[block, pl.ds(h * part_rows, part_rows), pl.ds(pl.multiple_of(p * width, 128), width)]

    def copy(block, p, h, own, send, device):
        src = tok.at[pl.ds(h * part_rows, part_rows), :] if own else piece(block, p, h)
        return pltpu.make_async_remote_copy(
            src_ref=src, dst_ref=piece(block, p, h), send_sem=send, recv_sem=recv.at[block, p, h],
            device_id=device, device_id_type=MESH)

    def right(p, h, own=False):
        return copy(b, p, h, own, z_send.at[0, p, h], {"tp": z + 1})

    def left(p, h, own=False):
        return copy(b, p, h, own, z_send.at[1, p, h], {"tp": z - 1})

    def across(j, p, h, own=False):
        return copy(b, p, h, own, x_send.at[j, p, h], {"ep": peers[j]})

    def to_core(block, p, h, own=False):
        return copy(block, p, h, own, c_send.at[block, p, h], {"ep": partner})

    def meta_copy(j):
        return pltpu.make_async_remote_copy(
            src_ref=meta, dst_ref=meta_out.at[b], send_sem=m_send.at[j], recv_sem=m_recv.at[b],
            device_id={"ep": others[j]}, device_id_type=MESH)

    local = pltpu.make_async_copy(tok, out.at[b, :, pl.ds(pl.multiple_of(z * width, 128), width)], local_sem.at[0])
    local_meta = pltpu.make_async_copy(meta, meta_out.at[b], local_sem.at[1])

    barrier = pltpu.get_barrier_semaphore()
    for other in others:
        pl.semaphore_signal(barrier, inc=1, device_id={"ep": other}, device_id_type=MESH)

    @pl.when(z > 0)
    def _():
        pl.semaphore_signal(barrier, inc=1, device_id={"tp": z - 1}, device_id_type=MESH)

    @pl.when(z < n_tp - 1)
    def _():
        pl.semaphore_signal(barrier, inc=1, device_id={"tp": z + 1}, device_id_type=MESH)

    pl.semaphore_wait(barrier, n_ep - 1 + jnp.minimum(z, 1) + jnp.minimum(n_tp - 1 - z, 1))

    def turn(block, way):
        return copy(block, z, 1, False, turn_send.at[way, block], {"tp": z + 1 - 2 * way})

    def fan_out(p, h, k):
        own = k == 0
        if not (k == 1 and h == 1):
            for j in range(chips - 1):
                across(j, p, h, own).start()
        to_core(b, p, h, own).start()

    for h in range(halves):
        @pl.when(z < n_tp - 1)
        def _():
            right(z, h, True).start()

        @pl.when(z > 0)
        def _():
            left(z, h, True).start()

        fan_out(z, h, 0)
    for j in range(n_ep - 1):
        meta_copy(j).start()
    local.start()
    local_meta.start()

    def pass_to_core(k, h):
        for p, there in ((z - k, z - k >= 0), (z + k, z + k < n_tp))[: 1 if k == 0 else 2]:
            @pl.when(there)
            def _():
                for block in peers:
                    to_core(block, p, h).wait_recv()
                    if k == 0 and h == 1:
                        @pl.when(z < n_tp - 1)
                        def _():
                            turn(block, 0).start()

                        @pl.when(z > 0)
                        def _():
                            turn(block, 1).start()

                    to_core(block, p, h).start()

    for k in range(1, n_tp):
        for h in range(halves):
            @pl.when(z - k >= 0)
            def _():
                right(z - k, h).wait_recv()

                @pl.when(z < n_tp - 1)
                def _():
                    right(z - k, h).start()

                fan_out(z - k, h, k)

            @pl.when(z + k < n_tp)
            def _():
                left(z + k, h).wait_recv()

                @pl.when(z > 0)
                def _():
                    left(z + k, h).start()

                fan_out(z + k, h, k)

            pass_to_core(k - 1, h)
    for h in range(halves):
        pass_to_core(n_tp - 1, h)

    for p in range(n_tp):
        for h in range(halves):
            for block in [partner] + [peer + partner - b for peer in peers]:
                to_core(block, p, h).wait_recv()
            for block in [b] + peers:
                to_core(block, p, h).wait_send()
            if h == 1:
                @pl.when((p != z - 1) & (p != z + 1))
                def _():
                    for j in range(chips - 1):
                        across(j, p, h).wait_send()
            else:
                for j in range(chips - 1):
                    across(j, p, h).wait_send()

            @pl.when((z < n_tp - 1) & (p <= z))
            def _():
                right(p, h).wait_send()

            @pl.when((z > 0) & (p >= z))
            def _():
                left(p, h).wait_send()
    if halves > 1:
        for block in peers:
            @pl.when(z < n_tp - 1)
            def _():
                turn(block, 0).wait_send()

            @pl.when(z > 0)
            def _():
                turn(block, 1).wait_send()

    for j in range(n_ep - 1):
        meta_copy(j).wait_send()
        pltpu.make_async_remote_copy(
            src_ref=meta, dst_ref=meta_out.at[others[j]], send_sem=m_send.at[j], recv_sem=m_recv.at[others[j]],
            device_id={"ep": others[j]}, device_id_type=MESH).wait_recv()
    local.wait()
    local_meta.wait()


def gather_tokens(tokens, meta, n_ep, n_tp):
    rows, width = tokens.shape
    halves = 2 if n_ep * n_tp <= 16 else 1
    dma = pltpu.SemaphoreType.DMA
    hbm = pl.BlockSpec(memory_space=pl.ANY)
    return pl.pallas_call(
        functools.partial(gather_kernel, n_ep, n_tp, halves),
        out_shape=(jax.ShapeDtypeStruct((n_ep, rows, n_tp * width), tokens.dtype),
                   jax.ShapeDtypeStruct((n_ep,) + meta.shape, meta.dtype)),
        in_specs=[hbm, hbm],
        out_specs=(hbm, hbm),
        scratch_shapes=[dma((2,)), dma((2, n_tp, halves)), dma((2, n_ep)), dma((max(1, n_ep // 2 - 1), n_tp, halves)),
                        dma((n_ep, n_tp, halves)), dma((n_ep, n_tp, halves)), dma((n_ep,)), dma((n_ep,))],
        compiler_params=pltpu.CompilerParams(collective_id=0, has_side_effects=True),
        name="gather_tokens",
    )(tokens, meta)


def ffn_kernel(n_ep, n_tp, cols, tokens, onehot, gate, up, down, ret, x, held, wg, wu, wd, hid, acc, done,
               t_sem, w_sem, d_sem, r_send, l_send, recv, b_send, b_recv, o_send, o_recv):
    z = lax.axis_index("tp")
    b = lax.axis_index("ep")
    chips = n_ep // 2
    others = [lax.rem(b + j, n_ep) for j in range(1, n_ep)]
    steps = hid.shape[1]
    depth = steps * cols
    width = x.shape[1]
    strip = width // 4

    def order(i):
        return 2 * lax.rem(b // 2 + 1 + i // 2, chips) + lax.rem(b + 1 + i, 2)

    def rows_of(block):
        return pl.ds(pl.multiple_of(block * CAP, 16), CAP)

    def fetch(c, slot):
        at = pl.ds(pl.multiple_of(c * cols, 128), cols)
        return (pltpu.make_async_copy(gate.at[:, at], wg.at[slot], w_sem.at[0, slot]),
                pltpu.make_async_copy(up.at[:, at], wu.at[slot], w_sem.at[1, slot]))

    def fetch_down(s):
        at = pl.ds(pl.multiple_of(s * depth, 128), depth)
        return pltpu.make_async_copy(down.at[at, :], wd.at[at, :], d_sem.at[s])

    def fetch_tokens(block, slot):
        return pltpu.make_async_copy(tokens.at[block], held.at[slot], t_sem.at[slot])

    def send(s, c, sem, to):
        return pltpu.make_async_remote_copy(
            src_ref=hid.at[s, c], dst_ref=hid.at[s, c], send_sem=sem.at[s, c], recv_sem=recv.at[s, c],
            device_id={"tp": to}, device_id_type=MESH)

    def right(s, c):
        return send(s, c, r_send, z + 1)

    def left(s, c):
        return send(s, c, l_send, z - 1)

    def block_send(s, block, way, to):
        at = hid.at[s, :, rows_of(block), :]
        return pltpu.make_async_remote_copy(
            src_ref=at, dst_ref=at, send_sem=b_send.at[way, block], recv_sem=b_recv.at[block],
            device_id={"tp": to}, device_id_type=MESH)

    def back(block, source):
        return pltpu.make_async_remote_copy(
            src_ref=done.at[block], dst_ref=ret.at[source], send_sem=o_send.at[block], recv_sem=o_recv.at[source],
            device_id={"ep": block}, device_id_type=MESH)

    fetch_tokens(0, 0).start()
    for copy in fetch(0, 0):
        copy.start()

    barrier = pltpu.get_barrier_semaphore()
    for other in others:
        pl.semaphore_signal(barrier, inc=1, device_id={"ep": other}, device_id_type=MESH)

    @pl.when(z > 0)
    def _():
        pl.semaphore_signal(barrier, inc=1, device_id={"tp": z - 1}, device_id_type=MESH)

    @pl.when(z < n_tp - 1)
    def _():
        pl.semaphore_signal(barrier, inc=1, device_id={"tp": z + 1}, device_id_type=MESH)

    @pl.loop(0, n_ep)
    def _(block):
        slot = lax.rem(block, 2)

        @pl.when(block + 1 < n_ep)
        def _():
            fetch_tokens(block + 1, 1 - slot).start()

        fetch_tokens(block, slot).wait()
        for j in range(4):
            at = pl.ds(j * strip, strip)
            x[rows_of(block), at] = jnp.dot(
                onehot[block], held[slot, :, at], preferred_element_type=jnp.float32).astype(x.dtype)

    acc[...] = jnp.zeros_like(acc)
    pl.semaphore_wait(barrier, n_ep - 1 + jnp.minimum(z, 1) + jnp.minimum(n_tp - 1 - z, 1))

    @pl.loop(0, steps)
    def _(c):
        slot = lax.rem(c, 2)

        @pl.when(c + 1 < steps)
        def _():
            for copy in fetch(c + 1, 1 - slot):
                copy.start()

        for copy in fetch(c, slot):
            copy.wait()
        pre_gate = jnp.dot(x[...], wg[slot], preferred_element_type=jnp.float32)
        pre_up = jnp.dot(x[...], wu[slot], preferred_element_type=jnp.float32)
        hid[z, c] = (pre_gate / (1.0 + jnp.exp(-pre_gate)) * pre_up).astype(hid.dtype)

        @pl.when(z < n_tp - 1)
        def _():
            right(z, c).start()

        @pl.when(z > 0)
        def _():
            left(z, c).start()

        @pl.when(c == max(0, steps - 2))
        def _():
            for s in range(n_tp):
                fetch_down(s).start()

    def weights_of(s, c):
        return wd[pl.ds(pl.multiple_of(s * depth + c * cols, 128), cols), :]

    def add(s, c):
        acc[...] += jnp.dot(hid[s, c], weights_of(s, c), preferred_element_type=jnp.float32)

    def add_at(k, c):
        if k == 0:
            add(z, c)
        else:
            @pl.when(z - k >= 0)
            def _():
                add(z - k, c)

            @pl.when(z + k < n_tp)
            def _():
                add(z + k, c)

    def finish(i):
        block = order(i)
        value = acc[rows_of(block), :].astype(ret.dtype)
        if i == n_ep - 1:
            ret[b] = value
        else:
            done[block] = value
            back(block, b).start()

    for k in range(1, n_tp - 1):
        @pl.loop(0, steps)
        def _(c):
            @pl.when(z - k >= 0)
            def _():
                right(z - k, c).wait_recv()

                @pl.when(z < n_tp - 1)
                def _():
                    if k < n_tp - 2:
                        right(z - k, c).start()
                    else:
                        @pl.when(c == steps - 1)
                        def _():
                            for i in range(n_ep):
                                block_send(z - k, order(i), 0, z + 1).start()

            @pl.when(z + k < n_tp)
            def _():
                left(z + k, c).wait_recv()

                @pl.when(z > 0)
                def _():
                    if k < n_tp - 2:
                        left(z + k, c).start()
                    else:
                        @pl.when(c == steps - 1)
                        def _():
                            for i in range(n_ep):
                                block_send(z + k, order(i), 1, z - 1).start()

            if k == 1:
                @pl.when(c == 0)
                def _():
                    for s in range(n_tp):
                        fetch_down(s).wait()

            add_at(k - 1, c)

    @pl.loop(0, steps)
    def _(c):
        add_at(n_tp - 2, c)

    at_end = (z == 0) | (z == n_tp - 1)

    @pl.when(at_end)
    def _():
        far = n_tp - 1 - z
        for i in range(n_ep):
            block = order(i)
            block_send(far, block, 0, jnp.where(z == 0, 1, z - 1)).wait_recv()

            @pl.loop(0, steps)
            def _(c):
                acc[rows_of(block), :] += jnp.dot(
                    hid[far, c, rows_of(block), :], weights_of(far, c), preferred_element_type=jnp.float32)

            finish(i)

    @pl.when(jnp.logical_not(at_end))
    def _():
        for i in range(n_ep):
            finish(i)

    @pl.loop(0, steps)
    def _(c):
        for s in range(n_tp):
            @pl.when((z < n_tp - 1) & (s <= z) & ((s > 0) | (z < n_tp - 2)))
            def _():
                right(s, c).wait_send()

            @pl.when((z > 0) & (s >= z) & ((s < n_tp - 1) | (z > 1)))
            def _():
                left(s, c).wait_send()

    for i in range(n_ep):
        @pl.when(z == n_tp - 2)
        def _():
            block_send(0, order(i), 0, z + 1).wait_send()

        @pl.when(z == 1)
        def _():
            block_send(n_tp - 1, order(i), 1, z - 1).wait_send()

    for other in others:
        back(other, other).wait_recv()
        back(other, b).wait_send()


def ffn(tokens, onehot, gate, up, down, n_ep, n_tp):
    width, hidden = gate.shape
    rows = n_ep * CAP
    out_width = down.shape[1]
    cols = min(256, hidden)
    steps = hidden // cols
    dma = pltpu.SemaphoreType.DMA
    hbm = pl.BlockSpec(memory_space=pl.ANY)
    vmem = pl.BlockSpec(memory_space=pltpu.VMEM)
    bf16 = jnp.bfloat16
    return pl.pallas_call(
        functools.partial(ffn_kernel, n_ep, n_tp, cols),
        out_shape=jax.ShapeDtypeStruct((n_ep, CAP, out_width), bf16),
        in_specs=[hbm, vmem, hbm, hbm, hbm],
        out_specs=vmem,
        scratch_shapes=[
            pltpu.VMEM((rows, width), bf16),
            pltpu.VMEM((2,) + tokens.shape[1:], bf16),
            pltpu.VMEM((2, width, cols), bf16), pltpu.VMEM((2, width, cols), bf16),
            pltpu.VMEM(down.shape, bf16),
            pltpu.VMEM((n_tp, steps, rows, cols), bf16),
            pltpu.VMEM((rows, out_width), jnp.float32),
            pltpu.VMEM((n_ep, CAP, out_width), bf16),
            dma((2,)), dma((2, 2)), dma((n_tp,)), dma((n_tp, steps)), dma((n_tp, steps)), dma((n_tp, steps)),
            dma((2, n_ep)), dma((n_ep,)), dma((n_ep,)), dma((n_ep,))],
        compiler_params=pltpu.CompilerParams(
            collective_id=1, has_side_effects=True, vmem_limit_bytes=60 * 1024 * 1024),
        cost_estimate=pl.CostEstimate(
            flops=2 * rows * (2 * width * hidden + down.size),
            bytes_accessed=2 * (gate.size + up.size + down.size), transcendentals=rows * hidden),
        name="ffn",
    )(tokens, onehot, gate, up, down)


def body(tokens, picks, gates, counts, gate_weight, up_weight, down_weight):
    n_ep, n_tp = lax.axis_size("ep"), lax.axis_size("tp")
    copies = n_ep // E
    row_count = tokens.shape[0]
    live = jnp.arange(row_count) < counts[0]
    meta = jnp.full((8, row_count), -1, jnp.int32).at[:2].set(jnp.where(live[None], picks.T, -1))
    gathered, meta_all = gather_tokens(tokens, meta, n_ep, n_tp)
    slots = jnp.arange(CAP, dtype=jnp.int32)

    expert = lax.axis_index("ep") // copies
    routed = jnp.any(meta_all[:, :2] == expert, axis=1)
    rank = jnp.cumsum(routed.astype(jnp.int32), axis=1) - 1
    onehot = (routed[:, None] & (rank[:, None] == slots[None, :, None])).astype(jnp.bfloat16)
    returned = ffn(gathered, onehot, gate_weight, up_weight, down_weight, n_ep, n_tp)

    matches = picks[:, :, None] == jnp.arange(E, dtype=jnp.int32)
    own_routed = jnp.any(matches, axis=1) & live[:, None]
    row_weight = jnp.sum(jnp.where(matches, gates[:, :, None], 0.0), axis=1)
    own_rank = jnp.cumsum(own_routed.astype(jnp.int32), axis=0) - 1
    placed = (own_routed.T[:, None] & (own_rank.T[:, None] == slots[None, :, None]))
    combine = placed.astype(jnp.float32) * row_weight.T[:, None, :]
    summed = jnp.sum(returned.reshape(E, copies, CAP, -1).astype(jnp.float32), axis=1)
    mixed = jnp.einsum("ecr,ecf->rf", combine, summed, precision=lax.Precision.HIGHEST)
    return mixed.astype(jnp.bfloat16)


def solution(mesh):
    rows = P(("groups", "ep"), None)
    in_specs = (
        P(("groups", "ep"), "tp"), rows, rows, P(("groups", "ep")),
        P(None, ("ep", "tp")), P(None, ("ep", "tp")), P("ep", "tp"),
    )
    out_specs = P(("groups", "ep"), "tp")
    return jax.shard_map(body, mesh=mesh, in_specs=in_specs, out_specs=out_specs, check_vma=False)
```

```python
import functools

import jax
import jax.numpy as jnp
from jax import lax
from jax.experimental import pallas as pl
from jax.experimental.pallas import tpu as pltpu
from jax.sharding import PartitionSpec as P

E = 4
CAP = 80
MESH = pl.DeviceIdType.MESH


def gather_kernel(n_ep, n_tp, halves, tok, meta, out, meta_out, local_sem, z_send, turn_send, x_send, c_send, recv, m_send, m_recv):
    z = lax.axis_index("tp")
    b = lax.axis_index("ep")
    chips = n_ep // 2
    rows, width = tok.shape
    part_rows = rows // halves
    partner = b + 1 - 2 * lax.rem(b, 2)
    peers = [2 * lax.rem(b // 2 + j, chips) + lax.rem(b, 2) for j in range(1, chips)]
    others = [lax.rem(b + j, n_ep) for j in range(1, n_ep)]

    def piece(block, p, h):
        return out.at[block, pl.ds(h * part_rows, part_rows), pl.ds(pl.multiple_of(p * width, 128), width)]

    def copy(block, p, h, own, send, device):
        src = tok.at[pl.ds(h * part_rows, part_rows), :] if own else piece(block, p, h)
        return pltpu.make_async_remote_copy(
            src_ref=src, dst_ref=piece(block, p, h), send_sem=send, recv_sem=recv.at[block, p, h],
            device_id=device, device_id_type=MESH)

    def right(p, h, own=False):
        return copy(b, p, h, own, z_send.at[0, p, h], {"tp": z + 1})

    def left(p, h, own=False):
        return copy(b, p, h, own, z_send.at[1, p, h], {"tp": z - 1})

    def across(j, p, h, own=False):
        return copy(b, p, h, own, x_send.at[j, p, h], {"ep": peers[j]})

    def to_core(block, p, h, own=False):
        return copy(block, p, h, own, c_send.at[block, p, h], {"ep": partner})

    def meta_copy(j):
        return pltpu.make_async_remote_copy(
            src_ref=meta, dst_ref=meta_out.at[b], send_sem=m_send.at[j], recv_sem=m_recv.at[b],
            device_id={"ep": others[j]}, device_id_type=MESH)

    local = pltpu.make_async_copy(tok, out.at[b, :, pl.ds(pl.multiple_of(z * width, 128), width)], local_sem.at[0])
    local_meta = pltpu.make_async_copy(meta, meta_out.at[b], local_sem.at[1])

    barrier = pltpu.get_barrier_semaphore()
    for other in others:
        pl.semaphore_signal(barrier, inc=1, device_id={"ep": other}, device_id_type=MESH)

    @pl.when(z > 0)
    def _():
        pl.semaphore_signal(barrier, inc=1, device_id={"tp": z - 1}, device_id_type=MESH)

    @pl.when(z < n_tp - 1)
    def _():
        pl.semaphore_signal(barrier, inc=1, device_id={"tp": z + 1}, device_id_type=MESH)

    pl.semaphore_wait(barrier, n_ep - 1 + jnp.minimum(z, 1) + jnp.minimum(n_tp - 1 - z, 1))

    def turn(block, way):
        return copy(block, z, 1, False, turn_send.at[way, block], {"tp": z + 1 - 2 * way})

    def fan_out(p, h, k):
        own = k == 0
        if not (k == 1 and h == 1):
            for j in range(chips - 1):
                across(j, p, h, own).start()
        to_core(b, p, h, own).start()

    for h in range(halves):
        @pl.when(z < n_tp - 1)
        def _():
            right(z, h, True).start()

        @pl.when(z > 0)
        def _():
            left(z, h, True).start()

        fan_out(z, h, 0)
    for j in range(n_ep - 1):
        meta_copy(j).start()
    local.start()
    local_meta.start()

    def pass_to_core(k, h):
        for p, there in ((z - k, z - k >= 0), (z + k, z + k < n_tp))[: 1 if k == 0 else 2]:
            @pl.when(there)
            def _():
                for block in peers:
                    to_core(block, p, h).wait_recv()
                    if k == 0 and h == 1:
                        @pl.when(z < n_tp - 1)
                        def _():
                            turn(block, 0).start()

                        @pl.when(z > 0)
                        def _():
                            turn(block, 1).start()

                    to_core(block, p, h).start()

    for k in range(1, n_tp):
        for h in range(halves):
            @pl.when(z - k >= 0)
            def _():
                right(z - k, h).wait_recv()

                @pl.when(z < n_tp - 1)
                def _():
                    right(z - k, h).start()

                fan_out(z - k, h, k)

            @pl.when(z + k < n_tp)
            def _():
                left(z + k, h).wait_recv()

                @pl.when(z > 0)
                def _():
                    left(z + k, h).start()

                fan_out(z + k, h, k)

        for h in range(halves):
            pass_to_core(k - 1, h)
    for h in range(halves):
        pass_to_core(n_tp - 1, h)

    for p in range(n_tp):
        for h in range(halves):
            for block in [partner] + [peer + partner - b for peer in peers]:
                to_core(block, p, h).wait_recv()
            for block in [b] + peers:
                to_core(block, p, h).wait_send()
            if h == 1:
                @pl.when((p != z - 1) & (p != z + 1))
                def _():
                    for j in range(chips - 1):
                        across(j, p, h).wait_send()
            else:
                for j in range(chips - 1):
                    across(j, p, h).wait_send()

            @pl.when((z < n_tp - 1) & (p <= z))
            def _():
                right(p, h).wait_send()

            @pl.when((z > 0) & (p >= z))
            def _():
                left(p, h).wait_send()
    if halves > 1:
        for block in peers:
            @pl.when(z < n_tp - 1)
            def _():
                turn(block, 0).wait_send()

            @pl.when(z > 0)
            def _():
                turn(block, 1).wait_send()

    for j in range(n_ep - 1):
        meta_copy(j).wait_send()
        pltpu.make_async_remote_copy(
            src_ref=meta, dst_ref=meta_out.at[others[j]], send_sem=m_send.at[j], recv_sem=m_recv.at[others[j]],
            device_id={"ep": others[j]}, device_id_type=MESH).wait_recv()
    local.wait()
    local_meta.wait()


def gather_tokens(tokens, meta, n_ep, n_tp):
    rows, width = tokens.shape
    halves = 2 if n_ep * n_tp <= 16 else 1
    dma = pltpu.SemaphoreType.DMA
    hbm = pl.BlockSpec(memory_space=pl.ANY)
    return pl.pallas_call(
        functools.partial(gather_kernel, n_ep, n_tp, halves),
        out_shape=(jax.ShapeDtypeStruct((n_ep, rows, n_tp * width), tokens.dtype),
                   jax.ShapeDtypeStruct((n_ep,) + meta.shape, meta.dtype)),
        in_specs=[hbm, hbm],
        out_specs=(hbm, hbm),
        scratch_shapes=[dma((2,)), dma((2, n_tp, halves)), dma((2, n_ep)), dma((max(1, n_ep // 2 - 1), n_tp, halves)),
                        dma((n_ep, n_tp, halves)), dma((n_ep, n_tp, halves)), dma((n_ep,)), dma((n_ep,))],
        compiler_params=pltpu.CompilerParams(collective_id=0, has_side_effects=True),
        name="gather_tokens",
    )(tokens, meta)


def ffn_kernel(n_ep, n_tp, cols, tokens, onehot, gate, up, down, ret, x, held, wg, wu, wd, hid, acc, done,
               t_sem, w_sem, d_sem, r_send, l_send, recv, b_send, b_recv, o_send, o_recv):
    z = lax.axis_index("tp")
    b = lax.axis_index("ep")
    chips = n_ep // 2
    others = [lax.rem(b + j, n_ep) for j in range(1, n_ep)]
    steps = hid.shape[1]
    depth = steps * cols
    width = x.shape[1]
    strip = width // 4

    def order(i):
        return 2 * lax.rem(b // 2 + 1 + i // 2, chips) + lax.rem(b + 1 + i, 2)

    def rows_of(block):
        return pl.ds(pl.multiple_of(block * CAP, 16), CAP)

    def fetch(c, slot):
        at = pl.ds(pl.multiple_of(c * cols, 128), cols)
        return (pltpu.make_async_copy(gate.at[:, at], wg.at[slot], w_sem.at[0, slot]),
                pltpu.make_async_copy(up.at[:, at], wu.at[slot], w_sem.at[1, slot]))

    def fetch_down(s):
        at = pl.ds(pl.multiple_of(s * depth, 128), depth)
        return pltpu.make_async_copy(down.at[at, :], wd.at[at, :], d_sem.at[s])

    def fetch_tokens(block, slot):
        return pltpu.make_async_copy(tokens.at[block], held.at[slot], t_sem.at[slot])

    def send(s, c, sem, to):
        return pltpu.make_async_remote_copy(
            src_ref=hid.at[s, c], dst_ref=hid.at[s, c], send_sem=sem.at[s, c], recv_sem=recv.at[s, c],
            device_id={"tp": to}, device_id_type=MESH)

    def right(s, c):
        return send(s, c, r_send, z + 1)

    def left(s, c):
        return send(s, c, l_send, z - 1)

    def block_send(s, block, way, to):
        at = hid.at[s, :, rows_of(block), :]
        return pltpu.make_async_remote_copy(
            src_ref=at, dst_ref=at, send_sem=b_send.at[way, block], recv_sem=b_recv.at[block],
            device_id={"tp": to}, device_id_type=MESH)

    def back(block, source):
        return pltpu.make_async_remote_copy(
            src_ref=done.at[block], dst_ref=ret.at[source], send_sem=o_send.at[block], recv_sem=o_recv.at[source],
            device_id={"ep": block}, device_id_type=MESH)

    fetch_tokens(0, 0).start()
    for copy in fetch(0, 0):
        copy.start()

    barrier = pltpu.get_barrier_semaphore()
    for other in others:
        pl.semaphore_signal(barrier, inc=1, device_id={"ep": other}, device_id_type=MESH)

    @pl.when(z > 0)
    def _():
        pl.semaphore_signal(barrier, inc=1, device_id={"tp": z - 1}, device_id_type=MESH)

    @pl.when(z < n_tp - 1)
    def _():
        pl.semaphore_signal(barrier, inc=1, device_id={"tp": z + 1}, device_id_type=MESH)

    @pl.loop(0, n_ep)
    def _(block):
        slot = lax.rem(block, 2)

        @pl.when(block + 1 < n_ep)
        def _():
            fetch_tokens(block + 1, 1 - slot).start()

        fetch_tokens(block, slot).wait()
        for j in range(4):
            at = pl.ds(j * strip, strip)
            x[rows_of(block), at] = jnp.dot(
                onehot[block], held[slot, :, at], preferred_element_type=jnp.float32).astype(x.dtype)

    acc[...] = jnp.zeros_like(acc)
    pl.semaphore_wait(barrier, n_ep - 1 + jnp.minimum(z, 1) + jnp.minimum(n_tp - 1 - z, 1))

    @pl.loop(0, steps)
    def _(c):
        slot = lax.rem(c, 2)

        @pl.when(c + 1 < steps)
        def _():
            for copy in fetch(c + 1, 1 - slot):
                copy.start()

        for copy in fetch(c, slot):
            copy.wait()
        pre_gate = jnp.dot(x[...], wg[slot], preferred_element_type=jnp.float32)
        pre_up = jnp.dot(x[...], wu[slot], preferred_element_type=jnp.float32)
        hid[z, c] = (pre_gate / (1.0 + jnp.exp(-pre_gate)) * pre_up).astype(hid.dtype)

        @pl.when(z < n_tp - 1)
        def _():
            right(z, c).start()

        @pl.when(z > 0)
        def _():
            left(z, c).start()

        @pl.when(c == max(0, steps - 2))
        def _():
            for s in range(n_tp):
                fetch_down(s).start()

    def weights_of(s, c):
        return wd[pl.ds(pl.multiple_of(s * depth + c * cols, 128), cols), :]

    def add(s, c):
        acc[...] += jnp.dot(hid[s, c], weights_of(s, c), preferred_element_type=jnp.float32)

    def add_at(k, c):
        if k == 0:
            add(z, c)
        else:
            @pl.when(z - k >= 0)
            def _():
                add(z - k, c)

            @pl.when(z + k < n_tp)
            def _():
                add(z + k, c)

    def finish(i):
        block = order(i)
        value = acc[rows_of(block), :].astype(ret.dtype)
        if i == n_ep - 1:
            ret[b] = value
        else:
            done[block] = value
            back(block, b).start()

    for k in range(1, n_tp - 1):
        @pl.loop(0, steps)
        def _(c):
            @pl.when(z - k >= 0)
            def _():
                right(z - k, c).wait_recv()

                @pl.when(z < n_tp - 1)
                def _():
                    if k < n_tp - 2:
                        right(z - k, c).start()
                    else:
                        @pl.when(c == steps - 1)
                        def _():
                            for i in range(n_ep):
                                block_send(z - k, order(i), 0, z + 1).start()

            @pl.when(z + k < n_tp)
            def _():
                left(z + k, c).wait_recv()

                @pl.when(z > 0)
                def _():
                    if k < n_tp - 2:
                        left(z + k, c).start()
                    else:
                        @pl.when(c == steps - 1)
                        def _():
                            for i in range(n_ep):
                                block_send(z + k, order(i), 1, z - 1).start()

            if k == 1:
                @pl.when(c == 0)
                def _():
                    for s in range(n_tp):
                        fetch_down(s).wait()

            add_at(k - 1, c)

    @pl.loop(0, steps)
    def _(c):
        add_at(n_tp - 2, c)

    at_end = (z == 0) | (z == n_tp - 1)

    @pl.when(at_end)
    def _():
        far = n_tp - 1 - z
        for i in range(n_ep):
            block = order(i)
            block_send(far, block, 0, jnp.where(z == 0, 1, z - 1)).wait_recv()

            @pl.loop(0, steps)
            def _(c):
                acc[rows_of(block), :] += jnp.dot(
                    hid[far, c, rows_of(block), :], weights_of(far, c), preferred_element_type=jnp.float32)

            finish(i)

    @pl.when(jnp.logical_not(at_end))
    def _():
        for i in range(n_ep):
            finish(i)

    @pl.loop(0, steps)
    def _(c):
        for s in range(n_tp):
            @pl.when((z < n_tp - 1) & (s <= z) & ((s > 0) | (z < n_tp - 2)))
            def _():
                right(s, c).wait_send()

            @pl.when((z > 0) & (s >= z) & ((s < n_tp - 1) | (z > 1)))
            def _():
                left(s, c).wait_send()

    for i in range(n_ep):
        @pl.when(z == n_tp - 2)
        def _():
            block_send(0, order(i), 0, z + 1).wait_send()

        @pl.when(z == 1)
        def _():
            block_send(n_tp - 1, order(i), 1, z - 1).wait_send()

    for other in others:
        back(other, other).wait_recv()
        back(other, b).wait_send()


def ffn(tokens, onehot, gate, up, down, n_ep, n_tp):
    width, hidden = gate.shape
    rows = n_ep * CAP
    out_width = down.shape[1]
    cols = min(256, hidden)
    steps = hidden // cols
    dma = pltpu.SemaphoreType.DMA
    hbm = pl.BlockSpec(memory_space=pl.ANY)
    vmem = pl.BlockSpec(memory_space=pltpu.VMEM)
    bf16 = jnp.bfloat16
    return pl.pallas_call(
        functools.partial(ffn_kernel, n_ep, n_tp, cols),
        out_shape=jax.ShapeDtypeStruct((n_ep, CAP, out_width), bf16),
        in_specs=[hbm, vmem, hbm, hbm, hbm],
        out_specs=vmem,
        scratch_shapes=[
            pltpu.VMEM((rows, width), bf16),
            pltpu.VMEM((2,) + tokens.shape[1:], bf16),
            pltpu.VMEM((2, width, cols), bf16), pltpu.VMEM((2, width, cols), bf16),
            pltpu.VMEM(down.shape, bf16),
            pltpu.VMEM((n_tp, steps, rows, cols), bf16),
            pltpu.VMEM((rows, out_width), jnp.float32),
            pltpu.VMEM((n_ep, CAP, out_width), bf16),
            dma((2,)), dma((2, 2)), dma((n_tp,)), dma((n_tp, steps)), dma((n_tp, steps)), dma((n_tp, steps)),
            dma((2, n_ep)), dma((n_ep,)), dma((n_ep,)), dma((n_ep,))],
        compiler_params=pltpu.CompilerParams(
            collective_id=1, has_side_effects=True, vmem_limit_bytes=60 * 1024 * 1024),
        cost_estimate=pl.CostEstimate(
            flops=2 * rows * (2 * width * hidden + down.size),
            bytes_accessed=2 * (gate.size + up.size + down.size), transcendentals=rows * hidden),
        name="ffn",
    )(tokens, onehot, gate, up, down)


def body(tokens, picks, gates, counts, gate_weight, up_weight, down_weight):
    n_ep, n_tp = lax.axis_size("ep"), lax.axis_size("tp")
    copies = n_ep // E
    row_count = tokens.shape[0]
    live = jnp.arange(row_count) < counts[0]
    meta = jnp.full((8, row_count), -1, jnp.int32).at[:2].set(jnp.where(live[None], picks.T, -1))
    gathered, meta_all = gather_tokens(tokens, meta, n_ep, n_tp)
    slots = jnp.arange(CAP, dtype=jnp.int32)

    expert = lax.axis_index("ep") // copies
    routed = jnp.any(meta_all[:, :2] == expert, axis=1)
    rank = jnp.cumsum(routed.astype(jnp.int32), axis=1) - 1
    onehot = (routed[:, None] & (rank[:, None] == slots[None, :, None])).astype(jnp.bfloat16)
    returned = ffn(gathered, onehot, gate_weight, up_weight, down_weight, n_ep, n_tp)

    matches = picks[:, :, None] == jnp.arange(E, dtype=jnp.int32)
    own_routed = jnp.any(matches, axis=1) & live[:, None]
    row_weight = jnp.sum(jnp.where(matches, gates[:, :, None], 0.0), axis=1)
    own_rank = jnp.cumsum(own_routed.astype(jnp.int32), axis=0) - 1
    placed = (own_routed.T[:, None] & (own_rank.T[:, None] == slots[None, :, None]))
    combine = placed.astype(jnp.float32) * row_weight.T[:, None, :]
    summed = jnp.sum(returned.reshape(E, copies, CAP, -1).astype(jnp.float32), axis=1)
    mixed = jnp.einsum("ecr,ecf->rf", combine, summed, precision=lax.Precision.HIGHEST)
    return mixed.astype(jnp.bfloat16)


def solution(mesh):
    rows = P(("groups", "ep"), None)
    in_specs = (
        P(("groups", "ep"), "tp"), rows, rows, P(("groups", "ep")),
        P(None, ("ep", "tp")), P(None, ("ep", "tp")), P("ep", "tp"),
    )
    out_specs = P(("groups", "ep"), "tp")
    return jax.shard_map(body, mesh=mesh, in_specs=in_specs, out_specs=out_specs, check_vma=False)
```
